256 devices in a mesh: island: 32 (over z_lo, y, core), fsdp: 8 (over x, z_hi).
Axes of the slice: x: 4, y: 4, z: 8 (z_hi: 2, z_lo: 4; z = z_hi * 4 + z_lo), core: 2. Of those that a mesh axis runs over, the one named last changes fastest.
Arguments:
- queries: bfloat16 [32, 2048, 2048], P('island', 'fsdp'), may hold values from -5 to 5
- keys: bfloat16 [32, 2048, 512], P('island', 'fsdp'), may hold values from -5 to 5
- values: bfloat16 [32, 2048, 512], P('island', 'fsdp'), may hold values from -6 to 6
- d_out: bfloat16 [32, 2048, 2048], P('island', 'fsdp'), may hold values from -6 to 6
- lengths: int32 [32], P('island'), may hold values from 256 to 2048
- steps: int32 [32], P('island'), may hold values from 50 to 100
- theta_global: float32 [768, 4096], P('fsdp'), may hold values from -6 to 6
- theta_local: bfloat16 [32, 768, 4096], P('island', 'fsdp'), may hold values from -6 to 6
- momentum: float32 [768, 4096], P('fsdp'), may hold values from -3 to 3
Outputs:
- context: bfloat16 [32, 2048, 2048], P('island', 'fsdp')
- d_queries: bfloat16 [32, 2048, 2048], P('island', 'fsdp')
- d_keys: bfloat16 [32, 2048, 512], P('island', 'fsdp')
- d_values: bfloat16 [32, 2048, 512], P('island', 'fsdp')
- theta_new: float32 [768, 4096], P('fsdp')
- momentum_new: float32 [768, 4096], P('fsdp')
The draws below stay inside these ranges and needn't reach their ends.
All inputs are finite; a program needn't handle non-finite values.
Results may differ from the reference program's by a relative error of at most 0.0033.
The reference program's roundings to bfloat16 on the way count: a program that leaves them out, or rounds other values in their place, can miss the bound.
Values may be sent and summed in bfloat16 or wider, within the bound.
No kernel may reach another device: no remote copies, remote signals or barrier semaphores. Data moves between devices by JAX's collectives and lax.ppermute only.
A program may use at most 192 MiB of HBM per device.

```python
import jax
import jax.numpy as jnp
from jax import lax

D = 4096
QUERY_HEADS = 16
KEY_VALUE_HEADS = 4
HEAD_SIZE = 128
STEPS_MAX = 100
SEQUENCE_LENGTH = 2048
ISLAND_COUNT = 32
FRAG = 768


def draw_queries(key, part):
    key = jax.random.fold_in(key, 1)
    complete_shape = (ISLAND_COUNT, SEQUENCE_LENGTH, QUERY_HEADS * HEAD_SIZE)
    return jnp.clip(1.5 * jax.random.normal(key, complete_shape, jnp.float32), -4.5, 4.5).astype(jnp.bfloat16)


def draw_keys(key, part):
    key = jax.random.fold_in(key, 2)
    complete_shape = (ISLAND_COUNT, SEQUENCE_LENGTH, KEY_VALUE_HEADS * HEAD_SIZE)
    return jnp.clip(1.4 * jax.random.normal(key, complete_shape, jnp.float32), -4.5, 4.5).astype(jnp.bfloat16)


def draw_lengths(key, part):
    key = jax.random.fold_in(key, 3)
    island_ids = jnp.arange(ISLAND_COUNT, dtype=jnp.int32)
    lowest = SEQUENCE_LENGTH // 8
    ramp_rows = lowest + (SEQUENCE_LENGTH - lowest) * island_ids // max(ISLAND_COUNT - 1, 1)
    jitter = jax.random.randint(key, (ISLAND_COUNT,), 0, SEQUENCE_LENGTH // 8 + 1)
    picked = jnp.clip(ramp_rows - jitter, lowest, SEQUENCE_LENGTH)
    picked = picked.at[0].set(lowest).at[ISLAND_COUNT - 1].set(SEQUENCE_LENGTH)
    return picked.astype(jnp.int32)


def draw_steps(key, part):
    key = jax.random.fold_in(key, 4)
    picked = jax.random.randint(key, (ISLAND_COUNT,), STEPS_MAX // 2, STEPS_MAX + 1)
    picked = picked.at[0].set(STEPS_MAX // 2).at[ISLAND_COUNT - 1].set(STEPS_MAX)
    return picked.astype(jnp.int32)


def steps_of(own_key, shape, split, low, largest):
    loudness, own = 1.0, jax.random.fold_in(own_key, 6)
    for axis_at, shards_of in split:
        steps = jnp.exp(jax.random.uniform(jax.random.fold_in(own, axis_at), (shards_of,), jnp.float32, low / len(split), largest / len(split)))
        loudness = loudness * jnp.repeat(steps, shape[axis_at] // shards_of).reshape([-1 if axis == axis_at else 1 for axis in range(len(shape))])
    return loudness


def centred(stream_key, shape, deviation, limit, pieces=(), kind=jnp.bfloat16):
    values = deviation * jax.random.normal(stream_key, shape, jnp.float32)
    if pieces:
        values = values * steps_of(stream_key, shape, pieces, -0.22, 0.18)
    return jnp.clip(values, -limit, limit).astype(kind)


def setup_inputs(seed: int = 0) -> dict:
    streams_of = jax.random.split(jax.random.key(seed), 10)
    return {
        "queries": draw_queries(jax.random.fold_in(streams_of[9], 71), 0),
        "keys": draw_keys(jax.random.fold_in(streams_of[9], 71), 0),
        "values": centred(streams_of[2], (ISLAND_COUNT, SEQUENCE_LENGTH, KEY_VALUE_HEADS * HEAD_SIZE), 1.0, 6.0, ((0, 32), (1, 8))),
        "d_out": centred(streams_of[3], (ISLAND_COUNT, SEQUENCE_LENGTH, QUERY_HEADS * HEAD_SIZE), 1.0, 6.0, ((0, 32), (1, 8))),
        "lengths": draw_lengths(jax.random.fold_in(streams_of[9], 71), 0),
        "steps": draw_steps(jax.random.fold_in(streams_of[9], 71), 0),
        "theta_global": centred(streams_of[6], (FRAG, D), 1.0, 6.0, ((0, 8),), jnp.float32),
        "theta_local": centred(streams_of[7], (ISLAND_COUNT, FRAG, D), 1.0, 6.0, ((0, 32), (1, 8))),
        "momentum": centred(streams_of[8], (FRAG, D), 0.5, 3.0, ((0, 8),), jnp.float32),
    }


neg_large = -1.0e30
outer_momentum = 0.9
outer_rate = 0.7


def to_bf16_f32(array_in):
    return lax.optimization_barrier(array_in.astype(jnp.bfloat16)).astype(jnp.float32)


def island_attention(operands):
    queries, keys, values, d_out, length = operands
    group_width = QUERY_HEADS // KEY_VALUE_HEADS
    score_scale = HEAD_SIZE ** -0.5
    query_head_rows = queries.reshape(SEQUENCE_LENGTH, QUERY_HEADS, HEAD_SIZE).astype(jnp.float32)
    key_head_rows = jnp.repeat(keys.reshape(SEQUENCE_LENGTH, KEY_VALUE_HEADS, HEAD_SIZE), group_width, axis=1).astype(jnp.float32)
    value_head_rows = jnp.repeat(values.reshape(SEQUENCE_LENGTH, KEY_VALUE_HEADS, HEAD_SIZE), group_width, axis=1).astype(jnp.float32)
    positions = jnp.arange(SEQUENCE_LENGTH, dtype=jnp.int32)
    allowed = (positions[None, :] <= positions[:, None]) & (positions[None, :] < length)
    scores = jnp.einsum("qhd,khd->hqk", query_head_rows, key_head_rows) * score_scale
    scores = jnp.where(allowed[None], scores, neg_large)
    row_max = jnp.max(scores, axis=2, keepdims=True)
    log_total = row_max + jnp.log(jnp.sum(jnp.exp(scores - row_max), axis=2, keepdims=True))
    soft_weights = jnp.exp(scores - log_total)
    soft_rounded = to_bf16_f32(soft_weights)
    context_full = jnp.einsum("hqk,khd->qhd", soft_rounded, value_head_rows)
    context = context_full.astype(jnp.bfloat16).reshape(SEQUENCE_LENGTH, QUERY_HEADS * HEAD_SIZE)
    live = (positions < length)[:, None]
    output_masked = jnp.where(live, d_out, jnp.zeros_like(d_out))
    head_masked = output_masked.reshape(SEQUENCE_LENGTH, QUERY_HEADS, HEAD_SIZE).astype(jnp.float32)
    row_dots = jnp.sum(head_masked * context_full, axis=2)
    prob_grad = jnp.einsum("qhd,khd->hqk", head_masked, value_head_rows)
    grad_rounded = to_bf16_f32(soft_weights * (prob_grad - row_dots.T[:, :, None]))
    query_grad = jnp.einsum("hqk,khd->qhd", grad_rounded, key_head_rows) * score_scale
    key_gradient = jnp.einsum("hqk,qhd->khd", grad_rounded, query_head_rows) * score_scale
    key_gradient = jnp.sum(key_gradient.reshape(SEQUENCE_LENGTH, KEY_VALUE_HEADS, group_width, HEAD_SIZE), axis=2)
    value_gradient = jnp.einsum("hqk,qhd->khd", soft_rounded, head_masked)
    value_gradient = jnp.sum(value_gradient.reshape(SEQUENCE_LENGTH, KEY_VALUE_HEADS, group_width, HEAD_SIZE), axis=2)
    return (context,
            query_grad.astype(jnp.bfloat16).reshape(SEQUENCE_LENGTH, QUERY_HEADS * HEAD_SIZE),
            key_gradient.astype(jnp.bfloat16).reshape(SEQUENCE_LENGTH, KEY_VALUE_HEADS * HEAD_SIZE),
            value_gradient.astype(jnp.bfloat16).reshape(SEQUENCE_LENGTH, KEY_VALUE_HEADS * HEAD_SIZE))


def reference(queries, keys, values, d_out, lengths, steps, theta_global, theta_local, momentum):
    context, d_queries, d_keys, d_values = lax.map(island_attention, (queries, keys, values, d_out, lengths))
    island_weight = steps.astype(jnp.float32) * lengths.astype(jnp.float32)

    def add_island(total, operands):
        local_rows, weight = operands
        return total + weight * (theta_global - local_rows.astype(jnp.float32)), None

    weighted_sum = lax.scan(add_island, jnp.zeros_like(theta_global), (theta_local, island_weight))[0]
    pseudo = weighted_sum / jnp.sum(island_weight)
    momentum_new = outer_momentum * momentum + pseudo
    theta_new = theta_global - outer_rate * (pseudo + outer_momentum * momentum_new)
    return context, d_queries, d_keys, d_values, theta_new, momentum_new
```

```python
import math
import jax
import jax.numpy as jnp
from jax import lax
from jax.experimental import pallas as pl
from jax.experimental.pallas import tpu as pltpu
from jax.sharding import PartitionSpec as P

HEAD = 128
GROUPS = 4
WIDE = 4
COLS = WIDE * HEAD
TILE = 256
neg_large = -1e30
score_scale = HEAD ** (-0.5)
exp2_scale = score_scale / math.log(2.0)
outer_momentum = 0.9
outer_rate = 0.7


def attend(place_ref, qg_ref, kv_ref, out_ref, dkv_ref,
           soft, q_rows, g_rows, q_cols, g_cols, k_cols, v_cols):
    step = pl.program_id(0)
    rows = qg_ref.shape[0]
    window = kv_ref.shape[0]
    tiles = window // TILE
    side, length = place_ref[0], place_ref[1]
    base = (2 * step + side) * rows
    full = jnp.minimum(base, length) // TILE
    live = jnp.minimum(base + rows, length + (TILE - 1)) // TILE

    @pl.when(step == 0)
    def _():
        dkv_ref[...] = jnp.zeros_like(dkv_ref)
        for j in range(tiles):
            span = slice(j * TILE, (j + 1) * TILE)
            k_cols[:, span] = kv_ref[span, :HEAD].astype(jnp.float32).T.astype(jnp.bfloat16)
            v_cols[:, span] = kv_ref[span, HEAD:].astype(jnp.float32).T.astype(jnp.bfloat16)

    row_id = base + lax.broadcasted_iota(jnp.int32, (rows, HEAD), 0)
    for h in range(WIDE):
        span = slice(h * rows, (h + 1) * rows)
        q_h = qg_ref[:, h * HEAD:(h + 1) * HEAD]
        g_h = qg_ref[:, COLS + h * HEAD:COLS + (h + 1) * HEAD]
        g_h = jnp.where(row_id < length, g_h.astype(jnp.float32), 0.0)
        q_rows[span, :] = q_h
        g_rows[span, :] = g_h.astype(jnp.bfloat16)
        q_cols[:, span] = q_h.astype(jnp.float32).T.astype(jnp.bfloat16)
        g_cols[:, span] = g_h.T.astype(jnp.bfloat16)

    def at(j):
        return pl.ds(pl.multiple_of(j * TILE, TILE), TILE)

    def held(j):
        return at(((j + side) % 2) * (tiles // 2) + j // 2)

    def score(j):
        return exp2_scale * jnp.dot(kv_ref[held(j), :HEAD], q_cols[...], preferred_element_type=jnp.float32)

    def score_full(j, top):
        s = score(j)
        soft[at(j), :] = s
        return jnp.maximum(top, jnp.max(s, axis=0, keepdims=True))

    def score_edge(j, top):
        s = score(j)
        key_pos = j * TILE + lax.broadcasted_iota(jnp.int32, (TILE, rows), 0)
        query_pos = base + lax.broadcasted_iota(jnp.int32, (TILE, rows), 1)
        keep = (key_pos <= query_pos) & (key_pos < length)
        s = jnp.where(jnp.concatenate([keep] * WIDE, axis=1), s, neg_large)
        soft[at(j), :] = s
        return jnp.maximum(top, jnp.max(s, axis=0, keepdims=True))

    top = jnp.full((1, WIDE * rows), neg_large, jnp.float32)
    top = lax.fori_loop(0, full, score_full, top)
    top = lax.fori_loop(full, live, score_edge, top)

    def weigh(j, total):
        e = jnp.exp2(soft[at(j), :] - top)
        soft[at(j), :] = e
        return total + jnp.sum(e, axis=0, keepdims=True)

    total = lax.fori_loop(0, live, weigh, jnp.zeros((1, WIDE * rows), jnp.float32))
    inverse = 1.0 / total

    def forward(j, context):
        p = soft[at(j), :] * inverse
        soft[at(j), :] = p
        p = p.astype(jnp.bfloat16)
        dkv_ref[held(j), HEAD:] += jnp.dot(p, g_rows[...], preferred_element_type=jnp.float32)
        return context + jnp.dot(v_cols[:, held(j)], p, preferred_element_type=jnp.float32)

    context = lax.fori_loop(0, live, forward, jnp.zeros((HEAD, WIDE * rows), jnp.float32))
    dots = jnp.sum(g_cols[...].astype(jnp.float32) * context, axis=0, keepdims=True)
    for h in range(WIDE):
        out_ref[:, h * HEAD:(h + 1) * HEAD] = context[:, h * rows:(h + 1) * rows].T.astype(jnp.bfloat16)

    def backward(j, q_grad):
        d = jnp.dot(kv_ref[held(j), HEAD:], g_cols[...], preferred_element_type=jnp.float32)
        d = (soft[at(j), :] * (d - dots)).astype(jnp.bfloat16)
        dkv_ref[held(j), :HEAD] += score_scale * jnp.dot(d, q_rows[...], preferred_element_type=jnp.float32)
        return q_grad + jnp.dot(k_cols[:, held(j)], d, preferred_element_type=jnp.float32)

    q_grad = lax.fori_loop(0, live, backward, jnp.zeros((HEAD, WIDE * rows), jnp.float32))
    for h in range(WIDE):
        lanes = slice(COLS + h * HEAD, COLS + (h + 1) * HEAD)
        out_ref[:, lanes] = (score_scale * q_grad[:, h * rows:(h + 1) * rows].T).astype(jnp.bfloat16)


def attention(place, qg, kv):
    blocks, rows, _ = qg.shape
    window = kv.shape[0]
    wide = WIDE * rows
    pairs = blocks * 2 * rows // TILE * blocks // 2 * WIDE
    return pl.pallas_call(
        attend,
        grid=(blocks,),
        in_specs=[
            pl.BlockSpec(memory_space=pltpu.SMEM),
            pl.BlockSpec((None, rows, 2 * COLS), lambda b: (b, 0, 0)),
            pl.BlockSpec((window, 2 * HEAD), lambda b: (0, 0)),
        ],
        out_specs=[
            pl.BlockSpec((None, rows, 2 * COLS), lambda b: (b, 0, 0)),
            pl.BlockSpec((window, 2 * HEAD), lambda b: (0, 0)),
        ],
        out_shape=[
            jax.ShapeDtypeStruct(qg.shape, jnp.bfloat16),
            jax.ShapeDtypeStruct((window, 2 * HEAD), jnp.float32),
        ],
        scratch_shapes=[
            pltpu.VMEM((window, wide), jnp.float32),
            pltpu.VMEM((wide, HEAD), jnp.bfloat16),
            pltpu.VMEM((wide, HEAD), jnp.bfloat16),
            pltpu.VMEM((HEAD, wide), jnp.bfloat16),
            pltpu.VMEM((HEAD, wide), jnp.bfloat16),
            pltpu.VMEM((HEAD, window), jnp.bfloat16),
            pltpu.VMEM((HEAD, window), jnp.bfloat16),
        ],
        compiler_params=pltpu.CompilerParams(vmem_limit_bytes=40 * 2**20),
        cost_estimate=pl.CostEstimate(
            flops=pairs * 10 * TILE * TILE * HEAD, bytes_accessed=8 * 2**20, transcendentals=pairs * TILE * TILE),
    )(place, qg, kv)


def body(queries, keys, values, d_out, lengths, steps, theta_global, theta_local, momentum):
    rows = queries.shape[1]
    key_width = keys.shape[2]
    ranks = lax.axis_size("fsdp")
    islands = lax.axis_size("island")
    across = [[2 * i + side for i in range(ranks // 2)] for side in range(2)]
    other = [(i, i ^ 1) for i in range(ranks)]
    side = lax.axis_index("fsdp") % 2
    place = jnp.stack([side.astype(jnp.int32), lengths[0]])

    def spread(x):
        return lax.all_to_all(x, "fsdp", 0, 0, axis_index_groups=across, tiled=True)

    def by_group(x):
        return jnp.transpose(x.reshape(rows, GROUPS, -1), (1, 0, 2))

    def by_row(x, width):
        return jnp.transpose(x, (1, 0, 2)).reshape(1, rows, width)

    kv = spread(jnp.concatenate([by_group(keys[0]), by_group(values[0])], axis=2))
    kv_other = lax.ppermute(kv, "fsdp", other)
    qg = spread(jnp.concatenate([by_group(queries[0]), by_group(d_out[0])], axis=2))
    window = 2 * GROUPS * rows
    out, part = attention(place, qg, jnp.concatenate([kv, kv_other], axis=0).reshape(window, 2 * HEAD))
    part = part.reshape(2, GROUPS, rows, 2 * HEAD)
    out = spread(out)
    context = by_row(out[:, :, :COLS], queries.shape[2])
    d_queries = by_row(out[:, :, COLS:], queries.shape[2])
    total = part[0] + lax.ppermute(part[1], "fsdp", other)
    grads = spread(total.astype(jnp.bfloat16))
    d_keys = by_row(grads[:, :, :HEAD], key_width)
    d_values = by_row(grads[:, :, HEAD:], key_width)

    frag_rows, width = theta_global.shape
    piece = width // islands
    note = jnp.stack([steps[0], lengths[0] // 16, lengths[0] % 16]).astype(jnp.bfloat16)
    note = jnp.broadcast_to(jnp.pad(note, (0, piece - 3)), (islands, 16, piece))
    local = jnp.transpose(theta_local[0].reshape(frag_rows, islands, piece), (1, 0, 2))
    local = lax.all_to_all(jnp.concatenate([local, note], axis=1), "island", 0, 0, tiled=True).astype(jnp.float32)
    note = local[:, frag_rows, :]
    weight = note[:, 0] * (16.0 * note[:, 1] + note[:, 2])
    mine = lax.dynamic_slice(theta_global, (0, lax.axis_index("island") * piece), (frag_rows, piece))
    pseudo = jnp.sum(weight[:, None, None] * (mine[None] - local[:, :frag_rows]), axis=0) / jnp.sum(weight)
    pseudo = lax.all_gather(pseudo, "island", axis=0)
    pseudo = jnp.transpose(pseudo, (1, 0, 2)).reshape(frag_rows, width)
    momentum_new = outer_momentum * momentum + pseudo
    theta_new = theta_global - outer_rate * (pseudo + outer_momentum * momentum_new)
    return (context, d_queries, d_keys, d_values, theta_new, momentum_new)


def solution(mesh):
    seq = P("island", "fsdp", None)
    return jax.shard_map(
        body,
        mesh=mesh,
        in_specs=(seq, seq, seq, seq, P("island"), P("island"), P("fsdp", None), seq, P("fsdp", None)),
        out_specs=(seq, seq, seq, seq, P("fsdp", None), P("fsdp", None)),
        check_vma=False,
    )
```

```python
import math
import jax
import jax.numpy as jnp
from jax import lax
from jax.experimental import pallas as pl
from jax.experimental.pallas import tpu as pltpu
from jax.sharding import PartitionSpec as P

HEAD = 128
GROUPS = 4
WIDE = 4
COLS = WIDE * HEAD
TILE = 512
NOTE = 16
neg_large = -1e30
score_scale = HEAD ** (-0.5)
exp2_scale = score_scale / math.log(2.0)
outer_momentum = 0.9
outer_rate = 0.7
f32 = jnp.float32
bf16 = jnp.bfloat16


def call(kernel, place, ins, outs, scratch=(), flops=0, exps=0, vmem=58):
    def whole(a):
        zeros = (0,) * len(a.shape)
        return pl.BlockSpec(a.shape, lambda: zeros)

    outs = [jax.ShapeDtypeStruct(s, t) for s, t in outs]
    size = sum(math.prod(a.shape) * a.dtype.itemsize for a in [*ins, *outs])
    return pl.pallas_call(
        kernel,
        in_specs=[pl.BlockSpec(memory_space=pltpu.SMEM)] + [whole(a) for a in ins],
        out_specs=[whole(a) for a in outs],
        out_shape=outs,
        scratch_shapes=[pltpu.VMEM(s, t) for s, t in scratch],
        compiler_params=pltpu.CompilerParams(vmem_limit_bytes=vmem * 2**20),
        cost_estimate=pl.CostEstimate(flops=flops, bytes_accessed=size if flops else 0, transcendentals=exps),
    )(place, *ins)


def after(earlier, later):
    return lax.optimization_barrier((earlier, later))[1]


def at(j):
    return pl.ds(pl.multiple_of(j * TILE, TILE), TILE)


def turn(x):
    return x.astype(f32).T.astype(bf16)


def source(place_ref, r):
    return (place_ref[0] + GROUPS - r) % GROUPS


def key_rows(place_ref, r, other):
    side = place_ref[1]
    block = 2 * source(place_ref, r) + ((1 - side) if other else side)
    return pl.ds(pl.multiple_of(block * (TILE // 2), TILE // 2), TILE // 2)


def lanes(index, width):
    return pl.ds(pl.multiple_of(index * width, width), width)


def extent(place_ref, r, rows):
    side, length = place_ref[1], place_ref[2]
    base = (2 * source(place_ref, r) + side) * rows
    live = (jnp.minimum(base + rows, length) + (TILE - 1)) // TILE
    return base, length, live


def keep_mask(j, base, length, rows):
    key_pos = j * TILE + lax.broadcasted_iota(jnp.int32, (TILE, rows), 0)
    query_pos = base + lax.broadcasted_iota(jnp.int32, (TILE, rows), 1)
    keep = (key_pos <= query_pos) & (key_pos < length)
    return jnp.concatenate([keep] * WIDE, axis=1)


def forward_kernel(place_ref, *refs):
    qg_refs, (near_ref, far_ref), refs = refs[:GROUPS], refs[GROUPS:GROUPS + 2], refs[GROUPS + 2:]
    ctx_refs, (near_out, far_out, stat_ref), refs = refs[:GROUPS], refs[GROUPS:GROUPS + 3], refs[GROUPS + 3:]
    soft, q_cols, g_cols, g_rows, v_cols, kv_ref, dv_ref = refs
    rows = qg_refs[0].shape[0]
    window = kv_ref.shape[0]
    wide = WIDE * rows
    dv_ref[...] = jnp.zeros_like(dv_ref)
    for r in range(GROUPS):
        kv_ref[key_rows(place_ref, r, False), :] = near_ref[r]
        kv_ref[key_rows(place_ref, r, True), :] = far_ref[r]
    for j in range(window // rows):
        span = slice(j * rows, (j + 1) * rows)
        v_cols[:, span] = turn(kv_ref[span, HEAD:])
    for r in range(GROUPS):
        base, length, live = extent(place_ref, r, rows)
        qg_ref = qg_refs[r]
        row_id = base + lax.broadcasted_iota(jnp.int32, (rows, HEAD), 0)
        for h in range(WIDE):
            span = slice(h * rows, (h + 1) * rows)
            g_h = qg_ref[:, COLS + h * HEAD:COLS + (h + 1) * HEAD]
            g_h = jnp.where(row_id < length, g_h.astype(f32), 0.0)
            g_rows[span, :] = g_h.astype(bf16)
            q_cols[:, span] = turn(qg_ref[:, h * HEAD:(h + 1) * HEAD])
            g_cols[:, span] = g_h.T.astype(bf16)

        def score(j):
            return exp2_scale * jnp.dot(kv_ref[at(j), :HEAD], q_cols[...], preferred_element_type=f32)

        def score_full(j, top):
            s = score(j)
            soft[at(j), :] = s
            return jnp.maximum(top, jnp.max(s, axis=0, keepdims=True))

        top = lax.fori_loop(0, live - 1, score_full, jnp.full((1, wide), neg_large, f32))
        s = jnp.where(keep_mask(live - 1, base, length, rows), score(live - 1), neg_large)
        soft[at(live - 1), :] = s
        top = jnp.maximum(top, jnp.max(s, axis=0, keepdims=True))

        def weigh(j, total):
            e = jnp.exp2(soft[at(j), :] - top)
            soft[at(j), :] = e
            return total + jnp.sum(e, axis=0, keepdims=True)

        total = lax.fori_loop(0, live, weigh, jnp.zeros((1, wide), f32))
        inverse = 1.0 / total

        def forward(j, context):
            p = (soft[at(j), :] * inverse).astype(bf16)
            dv_ref[at(j), :] += jnp.dot(p, g_rows[...], preferred_element_type=f32)
            return context + jnp.dot(v_cols[:, at(j)], p, preferred_element_type=f32)

        context = lax.fori_loop(0, live, forward, jnp.zeros((HEAD, wide), f32))
        stat_ref[r, 0:1, :] = top
        stat_ref[r, 1:2, :] = inverse
        stat_ref[r, 2:3, :] = jnp.sum(g_cols[...].astype(f32) * context, axis=0, keepdims=True)
        for h in range(WIDE):
            ctx_refs[r][:, h * HEAD:(h + 1) * HEAD] = context[:, h * rows:(h + 1) * rows].T.astype(bf16)
    for r in range(GROUPS):
        near_out[r] = dv_ref[key_rows(place_ref, r, False), :]
        far_out[r] = dv_ref[key_rows(place_ref, r, True), :].astype(bf16)


def backward_kernel(place_ref, *refs):
    qg_refs, (near_ref, far_ref, stat_ref), refs = refs[:GROUPS], refs[GROUPS:GROUPS + 3], refs[GROUPS + 3:]
    dq_refs, (near_out, far_out), refs = refs[:GROUPS], refs[GROUPS:GROUPS + 2], refs[GROUPS + 2:]
    q_cols, g_cols, q_rows, k_cols, dq_cols, kv_ref, dk_ref = refs
    rows = qg_refs[0].shape[0]
    window = kv_ref.shape[0]
    dk_ref[...] = jnp.zeros_like(dk_ref)
    for r in range(GROUPS):
        kv_ref[key_rows(place_ref, r, False), :] = near_ref[r]
        kv_ref[key_rows(place_ref, r, True), :] = far_ref[r]
    for j in range(window // rows):
        span = slice(j * rows, (j + 1) * rows)
        k_cols[:, span] = turn(kv_ref[span, :HEAD])
    for r in range(GROUPS):
        base, length, live = extent(place_ref, r, rows)
        qg_ref = qg_refs[r]
        row_id = base + lax.broadcasted_iota(jnp.int32, (rows, HEAD), 0)
        for h in range(WIDE):
            span = slice(h * rows, (h + 1) * rows)
            q_h = qg_ref[:, h * HEAD:(h + 1) * HEAD]
            g_h = qg_ref[:, COLS + h * HEAD:COLS + (h + 1) * HEAD]
            g_h = jnp.where(row_id < length, g_h.astype(f32), 0.0)
            q_rows[span, :] = q_h
            q_cols[:, span] = turn(q_h)
            g_cols[:, span] = g_h.T.astype(bf16)

        def backward(j, edge):
            s = exp2_scale * jnp.dot(kv_ref[at(j), :HEAD], q_cols[...], preferred_element_type=f32)
            if edge:
                s = jnp.where(keep_mask(j, base, length, rows), s, neg_large)
            p = jnp.exp2(s - stat_ref[r, 0:1, :]) * stat_ref[r, 1:2, :]
            d = jnp.dot(kv_ref[at(j), HEAD:], g_cols[...], preferred_element_type=f32)
            d = (p * (d - stat_ref[r, 2:3, :])).astype(bf16)
            dk_ref[at(j), :] += score_scale * jnp.dot(d, q_rows[...], preferred_element_type=f32)
            return jnp.dot(k_cols[:, at(j)], d, preferred_element_type=f32)

        dq_cols[...] = backward(live - 1, True)

        def step(j, carry):
            dq_cols[...] += backward(j, False)
            return carry

        lax.fori_loop(0, live - 1, step, 0)
        for h in range(WIDE):
            dq_refs[r][:, h * HEAD:(h + 1) * HEAD] = (score_scale * dq_cols[:, h * rows:(h + 1) * rows].T).astype(bf16)
    for r in range(GROUPS):
        near_out[r] = dk_ref[key_rows(place_ref, r, False), :]
        far_out[r] = dk_ref[key_rows(place_ref, r, True), :].astype(bf16)


def forward_call(place, blocks, near, far):
    groups, rows, _ = near.shape
    window, wide = 2 * groups * rows, WIDE * rows
    near_part, far_part = ((groups, rows, HEAD), f32), ((groups, rows, HEAD), bf16)
    return call(
        forward_kernel, place, [*blocks, near, far],
        [((rows, COLS), bf16)] * groups + [near_part, far_part, ((groups, 8, wide), f32)],
        [((window, wide), f32), ((HEAD, wide), bf16), ((HEAD, wide), bf16), ((wide, HEAD), bf16), ((HEAD, window), bf16),
         ((window, 2 * HEAD), bf16), ((window, HEAD), f32)],
        flops=12 * 10**9, exps=10**7, vmem=58)


def backward_call(place, blocks, near, far, stat):
    groups, rows, _ = near.shape
    window, wide = 2 * groups * rows, WIDE * rows
    near_part, far_part = ((groups, rows, HEAD), f32), ((groups, rows, HEAD), bf16)
    return call(
        backward_kernel, place, [*blocks, near, far, stat],
        [((rows, COLS), bf16)] * groups + [near_part, far_part],
        [((HEAD, wide), bf16), ((HEAD, wide), bf16), ((wide, HEAD), bf16), ((HEAD, window), bf16), ((HEAD, wide), f32),
         ((window, 2 * HEAD), bf16), ((window, HEAD), f32)],
        flops=12 * 10**9, exps=10**7, vmem=58)


def pack_kernel(place_ref, k_ref, v_ref, q_ref, g_ref, local_ref, note_ref, *refs):
    pair_refs, block_refs, sent_ref = refs[:GROUPS], refs[GROUPS:2 * GROUPS], refs[2 * GROUPS]
    for out_refs, ins, width in ((pair_refs, (k_ref, v_ref), HEAD), (block_refs, (q_ref, g_ref), COLS)):
        for r in range(GROUPS):
            for i, ref in enumerate(ins):
                out_refs[r][:, i * width:(i + 1) * width] = ref[:, lanes((place_ref[0] + r) % GROUPS, width)]
    width = sent_ref.shape[2]
    for i in range(sent_ref.shape[0]):
        sent_ref[i, :-NOTE, :] = local_ref[:, i * width:(i + 1) * width]
        sent_ref[i, -NOTE:, :] = note_ref[...]


def pack(place, k, v, q, g, local, note):
    rows, (note_rows, line) = k.shape[0], note.shape
    return call(
        pack_kernel, place, [k, v, q, g, local, note],
        [((rows, 2 * HEAD), bf16)] * GROUPS + [((rows, 2 * COLS), bf16)] * GROUPS
        + [((local.shape[1] // line, local.shape[0] + note_rows, line), bf16)])


def unpack_kernel(place_ref, *refs):
    ins, outs = refs[:GROUPS], refs[GROUPS:]
    width = outs[0].shape[1] // GROUPS
    for r in range(GROUPS):
        for i, out in enumerate(outs):
            out[:, lanes((place_ref[0] + r) % GROUPS, width)] = ins[r][:, i * width:(i + 1) * width]


def unpack(place, blocks, count):
    rows, width = blocks[0].shape
    return call(unpack_kernel, place, blocks, [((rows, GROUPS * width // count), bf16)] * count)


def merge_kernel(place_ref, dk_near, dk_far, dv_near, dv_far, *out_refs):
    for r in range(GROUPS):
        out_refs[r][:, :HEAD] = (dk_near[r] + dk_far[r].astype(f32)).astype(bf16)
        out_refs[r][:, HEAD:] = (dv_near[r] + dv_far[r].astype(f32)).astype(bf16)


def theta_sum_kernel(place_ref, g_ref, in_ref, out_ref):
    frag_rows, (count, _, width) = g_ref.shape[0], out_ref.shape
    for part in range(count):
        span = slice(part * width, (part + 1) * width)
        g = g_ref[:, lanes(place_ref[3] * count + part, width)]
        total, drift = 0.0, 0.0
        for i in range(in_ref.shape[0]):
            note = in_ref[i, frag_rows:, span].astype(f32)
            weight = note[0:1, :] * (16.0 * note[1:2, :] + note[2:3, :])
            total = total + weight
            drift = drift + weight * (g - in_ref[i, :frag_rows, span].astype(f32))
        out_ref[part, :frag_rows, :] = drift
        out_ref[part, frag_rows:, :] = jnp.broadcast_to(total, (8, width))


def theta_mean_kernel(place_ref, in_ref, out_ref):
    total = (in_ref[0] + in_ref[1]) + (in_ref[2] + in_ref[3])
    mean = total[:-8] / total[-8:-7]
    for part in range(out_ref.shape[0]):
        out_ref[part] = mean


def theta_update_kernel(place_ref, near_ref, far_ref, g_ref, m_ref, theta_ref, moment_ref):
    count, _, width = near_ref.shape
    for c, ref in ((place_ref[4], near_ref), (1 - place_ref[4], far_ref)):
        for k in range(count):
            z, y = divmod(k, 4)
            span = lanes((2 * y + c) * 4 + z, width)
            pseudo = ref[k]
            moment = outer_momentum * m_ref[:, span] + pseudo
            moment_ref[:, span] = moment
            theta_ref[:, span] = g_ref[:, span] - outer_rate * (pseudo + outer_momentum * moment)


def body(queries, keys, values, d_out, lengths, steps, theta_global, theta_local, momentum):
    rows = queries.shape[1]
    ranks, islands = lax.axis_size("fsdp"), lax.axis_size("island")
    rank = lax.axis_index("fsdp").astype(jnp.int32)
    me = lax.axis_index("island").astype(jnp.int32)
    place = jnp.stack([rank // 2, rank % 2, lengths[0], me % 8, me % 2])

    def along(x, r):
        return x if r == 0 else lax.ppermute(x, "fsdp", [(i, (i + 2 * r) % ranks) for i in range(ranks)])

    def back(blocks):
        return [along(x, -r) for r, x in enumerate(blocks)]

    def across(x):
        return lax.ppermute(x, "fsdp", [(i, i ^ 1) for i in range(ranks)])

    over_y_core = [[8 * z + i for i in range(8)] for z in range(4)]
    over_z = [[8 * z + i for z in range(4)] for i in range(8)]
    over_z_y = [[8 * z + 2 * y + c for z in range(4) for y in range(4)] for c in range(2)]

    def spread(x, groups):
        return lax.all_to_all(x, "island", 0, 0, axis_index_groups=groups, tiled=True)

    frag_rows, frag_width = theta_global.shape
    line, piece = frag_width // 8, frag_width // 32
    note = jnp.stack([steps[0], lengths[0] // 16, lengths[0] % 16]).astype(bf16)
    note = jnp.broadcast_to(jnp.pad(note, (0, NOTE - 3))[:, None], (NOTE, line))

    *packed, sent = pack(place, keys[0], values[0], queries[0], d_out[0], theta_local[0], note)
    drift = spread(sent, over_y_core)
    near, blocks = [along(x, r) for r, x in enumerate(packed[:GROUPS])], packed[GROUPS:]
    blocks[1] = along(blocks[1], 1)
    near, blocks[1] = lax.optimization_barrier((near, blocks[1]))
    near = jnp.stack(near)
    far = across(near)
    blocks[2], blocks[3] = after(near, (blocks[2], blocks[3]))
    blocks[2], blocks[3] = along(blocks[2], 2), along(blocks[3], 3)
    drift, = call(theta_sum_kernel, place, [theta_global, drift], [((4, frag_rows + 8, piece), f32)])
    blocks, near, far = after(drift, (blocks, near, far))
    drift = spread(drift, over_z)

    *context, v_near, v_far, stat = forward_call(place, blocks, near, far)
    v_far, drift, context, stat = lax.optimization_barrier((v_far, drift, context, stat))
    v_got = across(v_far)
    context = back(context)
    pseudo, = call(theta_mean_kernel, place, [drift], [((16, frag_rows, piece), f32)])
    stat = after(pseudo, stat)
    pseudo = spread(pseudo, over_z_y)
    *d_queries, k_near, k_far = backward_call(place, blocks, near, far, stat)
    k_far, v_got, context, pseudo = lax.optimization_barrier((k_far, v_got, context, pseudo))
    k_got = across(k_far)
    d_queries = back(d_queries)
    context = after(d_queries, context)
    context, = unpack(place, context, 1)
    k_got, pseudo = after(context, (k_got, pseudo))
    grads = call(merge_kernel, place, [k_near, k_got, v_near, v_got], [((rows, 2 * HEAD), bf16)] * GROUPS)
    grads_in = back(grads)
    pseudo = after(grads[0], pseudo)
    theta_far = lax.ppermute(pseudo, "island", [(i, i ^ 1) for i in range(islands)])
    d_queries, = unpack(place, after(grads[0], d_queries), 1)
    theta_new, momentum_new = call(
        theta_update_kernel, place, [pseudo, after(d_queries, theta_far), theta_global, momentum],
        [((frag_rows, frag_width), f32)] * 2)
    d_keys, d_values = unpack(place, after(theta_new, grads_in), 2)
    return (context[None], d_queries[None], d_keys[None], d_values[None], theta_new, momentum_new)


def solution(mesh):
    seq = P("island", "fsdp", None)
    return jax.shard_map(
        body,
        mesh=mesh,
        in_specs=(seq, seq, seq, seq, P("island"), P("island"), P("fsdp", None), seq, P("fsdp", None)),
        out_specs=(seq, seq, seq, seq, P("fsdp", None), P("fsdp", None)),
        check_vma=False,
    )
```

```python
import math
import jax
import jax.numpy as jnp
from jax import lax
from jax.experimental import pallas as pl
from jax.experimental.pallas import tpu as pltpu
from jax.sharding import PartitionSpec as P

HEAD = 128
GROUPS = 4
WIDE = 4
COLS = WIDE * HEAD
TILE = 512
NOTE = 16
neg_large = -1e30
score_scale = HEAD ** (-0.5)
exp2_scale = score_scale / math.log(2.0)
outer_momentum = 0.9
outer_rate = 0.7
f32 = jnp.float32
bf16 = jnp.bfloat16


def call(kernel, place, ins, outs, scratch=(), flops=0, exps=0, vmem=58):
    def whole(a):
        zeros = (0,) * len(a.shape)
        return pl.BlockSpec(a.shape, lambda: zeros)

    outs = [jax.ShapeDtypeStruct(s, t) for s, t in outs]
    size = sum(math.prod(a.shape) * a.dtype.itemsize for a in [*ins, *outs])
    return pl.pallas_call(
        kernel,
        in_specs=[pl.BlockSpec(memory_space=pltpu.SMEM)] + [whole(a) for a in ins],
        out_specs=[whole(a) for a in outs],
        out_shape=outs,
        scratch_shapes=[pltpu.VMEM(s, t) for s, t in scratch],
        compiler_params=pltpu.CompilerParams(vmem_limit_bytes=vmem * 2**20),
        cost_estimate=pl.CostEstimate(flops=flops, bytes_accessed=size if flops else 0, transcendentals=exps),
    )(place, *ins)


def after(earlier, later):
    return lax.optimization_barrier((earlier, later))[1]


def at(j):
    return pl.ds(pl.multiple_of(j * TILE, TILE), TILE)


def turn(x):
    return x.astype(f32).T.astype(bf16)


def source(place_ref, r):
    return (place_ref[0] + GROUPS - r) % GROUPS


def key_rows(place_ref, r, other):
    side = place_ref[1]
    block = 2 * source(place_ref, r) + ((1 - side) if other else side)
    return pl.ds(pl.multiple_of(block * (TILE // 2), TILE // 2), TILE // 2)


def lanes(index, width):
    return pl.ds(pl.multiple_of(index * width, width), width)


def extent(place_ref, r, rows):
    side, length = place_ref[1], place_ref[2]
    base = (2 * source(place_ref, r) + side) * rows
    live = (jnp.minimum(base + rows, length) + (TILE - 1)) // TILE
    return base, length, live


def keep_mask(j, base, length, rows):
    key_pos = j * TILE + lax.broadcasted_iota(jnp.int32, (TILE, rows), 0)
    query_pos = base + lax.broadcasted_iota(jnp.int32, (TILE, rows), 1)
    keep = (key_pos <= query_pos) & (key_pos < length)
    return jnp.concatenate([keep] * WIDE, axis=1)


def forward_kernel(place_ref, *refs):
    qg_refs, (near_ref, far_ref), refs = refs[:GROUPS], refs[GROUPS:GROUPS + 2], refs[GROUPS + 2:]
    ctx_refs, (near_out, far_out, stat_ref), refs = refs[:GROUPS], refs[GROUPS:GROUPS + 3], refs[GROUPS + 3:]
    soft, q_cols, g_cols, g_rows, v_cols, kv_ref, dv_ref, acc = refs
    rows = qg_refs[0].shape[0]
    window = kv_ref.shape[0]
    wide = WIDE * rows
    dv_ref[...] = jnp.zeros_like(dv_ref)
    for r in range(GROUPS):
        kv_ref[key_rows(place_ref, r, False), :] = near_ref[r]
        kv_ref[key_rows(place_ref, r, True), :] = far_ref[r]
    for j in range(window // rows):
        span = slice(j * rows, (j + 1) * rows)
        v_cols[:, span] = turn(kv_ref[span, HEAD:])
    for r in range(GROUPS):
        base, length, live = extent(place_ref, r, rows)
        qg_ref = qg_refs[r]
        row_id = base + lax.broadcasted_iota(jnp.int32, (rows, HEAD), 0)
        for h in range(WIDE):
            span = slice(h * rows, (h + 1) * rows)
            g_h = qg_ref[:, COLS + h * HEAD:COLS + (h + 1) * HEAD]
            g_h = jnp.where(row_id < length, g_h.astype(f32), 0.0)
            g_rows[span, :] = g_h.astype(bf16)
            q_cols[:, span] = turn(qg_ref[:, h * HEAD:(h + 1) * HEAD])
            g_cols[:, span] = g_h.T.astype(bf16)

        def score(j):
            return exp2_scale * jnp.dot(kv_ref[at(j), :HEAD], q_cols[...], preferred_element_type=f32)

        def score_full(j, top):
            s = score(j)
            soft[at(j), :] = s
            return jnp.maximum(top, jnp.max(s, axis=0, keepdims=True))

        top = lax.fori_loop(0, live - 1, score_full, jnp.full((1, wide), neg_large, f32))
        s = jnp.where(keep_mask(live - 1, base, length, rows), score(live - 1), neg_large)
        soft[at(live - 1), :] = s
        top = jnp.maximum(top, jnp.max(s, axis=0, keepdims=True))

        def weigh(j, total):
            e = jnp.exp2(soft[at(j), :] - top)
            soft[at(j), :] = e
            return total + jnp.sum(e, axis=0, keepdims=True)

        total = lax.fori_loop(0, live, weigh, jnp.zeros((1, wide), f32))
        inverse = 1.0 / total

        def forward(j, context):
            p = (soft[at(j), :] * inverse).astype(bf16)
            dv_ref[at(j), :] += jnp.dot(p, g_rows[...], preferred_element_type=f32)
            acc[...] += jnp.dot(v_cols[:, at(j)], p, preferred_element_type=f32)
            return context

        acc[...] = jnp.zeros_like(acc)
        lax.fori_loop(0, live, forward, 0)
        context = acc[...]
        stat_ref[r, 0:1, :] = top
        stat_ref[r, 1:2, :] = inverse
        stat_ref[r, 2:3, :] = jnp.sum(g_cols[...].astype(f32) * context, axis=0, keepdims=True)
        for h in range(WIDE):
            ctx_refs[r][:, h * HEAD:(h + 1) * HEAD] = context[:, h * rows:(h + 1) * rows].T.astype(bf16)
    for r in range(GROUPS):
        near_out[r] = dv_ref[key_rows(place_ref, r, False), :]
        far_out[r] = dv_ref[key_rows(place_ref, r, True), :].astype(bf16)


def backward_kernel(place_ref, *refs):
    qg_refs, (near_ref, far_ref, stat_ref), refs = refs[:GROUPS], refs[GROUPS:GROUPS + 3], refs[GROUPS + 3:]
    dq_refs, (near_out, far_out), refs = refs[:GROUPS], refs[GROUPS:GROUPS + 2], refs[GROUPS + 2:]
    q_cols, g_cols, q_rows, k_cols, dq_cols, kv_ref, dk_ref = refs
    rows = qg_refs[0].shape[0]
    window = kv_ref.shape[0]
    dk_ref[...] = jnp.zeros_like(dk_ref)
    for r in range(GROUPS):
        kv_ref[key_rows(place_ref, r, False), :] = near_ref[r]
        kv_ref[key_rows(place_ref, r, True), :] = far_ref[r]
    for j in range(window // rows):
        span = slice(j * rows, (j + 1) * rows)
        k_cols[:, span] = turn(kv_ref[span, :HEAD])
    for r in range(GROUPS):
        base, length, live = extent(place_ref, r, rows)
        qg_ref = qg_refs[r]
        row_id = base + lax.broadcasted_iota(jnp.int32, (rows, HEAD), 0)
        for h in range(WIDE):
            span = slice(h * rows, (h + 1) * rows)
            q_h = qg_ref[:, h * HEAD:(h + 1) * HEAD]
            g_h = qg_ref[:, COLS + h * HEAD:COLS + (h + 1) * HEAD]
            g_h = jnp.where(row_id < length, g_h.astype(f32), 0.0)
            q_rows[span, :] = q_h
            q_cols[:, span] = turn(q_h)
            g_cols[:, span] = g_h.T.astype(bf16)

        def backward(j, edge):
            s = exp2_scale * jnp.dot(kv_ref[at(j), :HEAD], q_cols[...], preferred_element_type=f32)
            if edge:
                s = jnp.where(keep_mask(j, base, length, rows), s, neg_large)
            p = jnp.exp2(s - stat_ref[r, 0:1, :]) * stat_ref[r, 1:2, :]
            d = jnp.dot(kv_ref[at(j), HEAD:], g_cols[...], preferred_element_type=f32)
            d = (p * (d - stat_ref[r, 2:3, :])).astype(bf16)
            dk_ref[at(j), :] += score_scale * jnp.dot(d, q_rows[...], preferred_element_type=f32)
            return jnp.dot(k_cols[:, at(j)], d, preferred_element_type=f32)

        dq_cols[...] = backward(live - 1, True)

        def step(j, carry):
            dq_cols[...] += backward(j, False)
            return carry

        lax.fori_loop(0, live - 1, step, 0)
        for h in range(WIDE):
            dq_refs[r][:, h * HEAD:(h + 1) * HEAD] = (score_scale * dq_cols[:, h * rows:(h + 1) * rows].T).astype(bf16)
    for r in range(GROUPS):
        near_out[r] = dk_ref[key_rows(place_ref, r, False), :]
        far_out[r] = dk_ref[key_rows(place_ref, r, True), :].astype(bf16)


def forward_call(place, blocks, near, far):
    groups, rows, _ = near.shape
    window, wide = 2 * groups * rows, WIDE * rows
    near_part, far_part = ((groups, rows, HEAD), f32), ((groups, rows, HEAD), bf16)
    return call(
        forward_kernel, place, [*blocks, near, far],
        [((rows, COLS), bf16)] * groups + [near_part, far_part, ((groups, 8, wide), f32)],
        [((window, wide), f32), ((HEAD, wide), bf16), ((HEAD, wide), bf16), ((wide, HEAD), bf16), ((HEAD, window), bf16),
         ((window, 2 * HEAD), bf16), ((window, HEAD), f32), ((HEAD, wide), f32)],
        flops=12 * 10**9, exps=10**7, vmem=58)


def backward_call(place, blocks, near, far, stat):
    groups, rows, _ = near.shape
    window, wide = 2 * groups * rows, WIDE * rows
    near_part, far_part = ((groups, rows, HEAD), f32), ((groups, rows, HEAD), bf16)
    return call(
        backward_kernel, place, [*blocks, near, far, stat],
        [((rows, COLS), bf16)] * groups + [near_part, far_part],
        [((HEAD, wide), bf16), ((HEAD, wide), bf16), ((wide, HEAD), bf16), ((HEAD, window), bf16), ((HEAD, wide), f32),
         ((window, 2 * HEAD), bf16), ((window, HEAD), f32)],
        flops=12 * 10**9, exps=10**7, vmem=58)


def pack_pairs_kernel(place_ref, a_ref, b_ref, *out_refs):
    width = a_ref.shape[1] // GROUPS
    for r in range(GROUPS):
        span = lanes((place_ref[0] + r) % GROUPS, width)
        out_refs[r][:, :width] = a_ref[:, span]
        out_refs[r][:, width:] = b_ref[:, span]


def pack_kernel(place_ref, q_ref, g_ref, local_ref, *refs):
    out_refs, sent_ref = refs[:GROUPS], refs[GROUPS]
    pack_pairs_kernel(place_ref, q_ref, g_ref, *out_refs)
    width = sent_ref.shape[2]
    row = lax.broadcasted_iota(jnp.int32, (NOTE, width), 0)
    length, steps = place_ref[2], place_ref[5]
    note = jnp.where(row == 0, steps, jnp.where(row == 1, length // 16, length % 16)).astype(f32).astype(bf16)
    for i in range(sent_ref.shape[0]):
        sent_ref[i, :-NOTE, :] = local_ref[:, i * width:(i + 1) * width]
        sent_ref[i, -NOTE:, :] = note


def pack_pairs(place, k, v):
    rows, width = k.shape
    return call(pack_pairs_kernel, place, [k, v], [((rows, 2 * width // GROUPS), bf16)] * GROUPS)


def pack(place, q, g, local):
    rows, (frag_rows, frag_width) = q.shape[0], local.shape
    return call(
        pack_kernel, place, [q, g, local],
        [((rows, 2 * COLS), bf16)] * GROUPS + [((8, frag_rows + NOTE, frag_width // 8), bf16)])


def unpack_kernel(place_ref, *refs):
    ins, outs = refs[:GROUPS], refs[GROUPS:]
    width = outs[0].shape[1] // GROUPS
    for r in range(GROUPS):
        for i, out in enumerate(outs):
            out[:, lanes((place_ref[0] + r) % GROUPS, width)] = ins[r][:, i * width:(i + 1) * width]


def unpack(place, blocks, count):
    rows, width = blocks[0].shape
    return call(unpack_kernel, place, blocks, [((rows, GROUPS * width // count), bf16)] * count)


def merge_kernel(place_ref, dk_near, dk_far, dv_near, dv_far, *out_refs):
    for r in range(GROUPS):
        out_refs[r][:, :HEAD] = (dk_near[r] + dk_far[r].astype(f32)).astype(bf16)
        out_refs[r][:, HEAD:] = (dv_near[r] + dv_far[r].astype(f32)).astype(bf16)


def theta_sum_kernel(place_ref, g_ref, in_ref, out_ref):
    frag_rows, (count, _, width) = g_ref.shape[0], out_ref.shape
    for part in range(count):
        span = slice(part * width, (part + 1) * width)
        g = g_ref[:, lanes(place_ref[3] * count + part, width)]
        total, drift = 0.0, 0.0
        for i in range(in_ref.shape[0]):
            note = in_ref[i, frag_rows:, span].astype(f32)
            weight = note[0:1, :] * (16.0 * note[1:2, :] + note[2:3, :])
            total = total + weight
            drift = drift + weight * (g - in_ref[i, :frag_rows, span].astype(f32))
        out_ref[part, :frag_rows, :] = drift
        out_ref[part, frag_rows:, :] = jnp.broadcast_to(total, (8, width))


def theta_mean_kernel(place_ref, in_ref, out_ref):
    total = (in_ref[0] + in_ref[1]) + (in_ref[2] + in_ref[3])
    mean = total[:-8] / total[-8:-7]
    for part in range(out_ref.shape[0]):
        out_ref[part] = mean


def theta_update_kernel(place_ref, near_ref, far_ref, g_ref, m_ref, theta_ref, moment_ref):
    count, _, width = near_ref.shape
    for c, ref in ((place_ref[4], near_ref), (1 - place_ref[4], far_ref)):
        for k in range(count):
            z, y = divmod(k, 4)
            span = lanes((2 * y + c) * 4 + z, width)
            pseudo = ref[k]
            moment = outer_momentum * m_ref[:, span] + pseudo
            moment_ref[:, span] = moment
            theta_ref[:, span] = g_ref[:, span] - outer_rate * (pseudo + outer_momentum * moment)


def body(queries, keys, values, d_out, lengths, steps, theta_global, theta_local, momentum):
    rows = queries.shape[1]
    ranks, islands = lax.axis_size("fsdp"), lax.axis_size("island")
    rank = lax.axis_index("fsdp").astype(jnp.int32)
    me = lax.axis_index("island").astype(jnp.int32)
    place = jnp.stack([rank // 2, rank % 2, lengths[0], me % 8, me % 2, steps[0]])

    def along(x, r):
        return x if r == 0 else lax.ppermute(x, "fsdp", [(i, (i + 2 * r) % ranks) for i in range(ranks)])

    def back(blocks):
        return [along(x, -r) for r, x in enumerate(blocks)]

    def across(x):
        return lax.ppermute(x, "fsdp", [(i, i ^ 1) for i in range(ranks)])

    over_y_core = [[8 * z + i for i in range(8)] for z in range(4)]
    over_z = [[8 * z + i for z in range(4)] for i in range(8)]
    over_z_y = [[8 * z + 2 * y + c for z in range(4) for y in range(4)] for c in range(2)]

    def spread(x, groups):
        return lax.all_to_all(x, "island", 0, 0, axis_index_groups=groups, tiled=True)

    frag_rows, frag_width = theta_global.shape
    line, piece = frag_width // 8, frag_width // 32
    near = [along(x, r) for r, x in enumerate(pack_pairs(place, keys[0], values[0]))]
    near, queries, d_out, theta_local = lax.optimization_barrier((near, queries, d_out, theta_local))
    near = jnp.stack(near)
    far = across(near)
    *blocks, sent = pack(place, queries[0], d_out[0], theta_local[0])
    blocks = [along(x, r) for r, x in enumerate(blocks)]
    drift = spread(sent, over_y_core)
    drift, = call(theta_sum_kernel, place, [theta_global, drift], [((4, frag_rows + 8, piece), f32)])
    blocks, near, far = after(drift, (blocks, near, far))
    drift = spread(drift, over_z)

    *context, v_near, v_far, stat = forward_call(place, blocks, near, far)
    v_far, drift, context, stat = lax.optimization_barrier((v_far, drift, context, stat))
    v_got = across(v_far)
    context = back(context)
    pseudo, = call(theta_mean_kernel, place, [drift], [((16, frag_rows, piece), f32)])
    stat = after(pseudo, stat)
    pseudo = spread(pseudo, over_z_y)
    *d_queries, k_near, k_far = backward_call(place, blocks, near, far, stat)
    k_far, v_got, context, pseudo = lax.optimization_barrier((k_far, v_got, context, pseudo))
    k_got = across(k_far)
    d_queries = back(d_queries)
    context = after(d_queries, context)
    context, = unpack(place, context, 1)
    k_got, pseudo = after(context, (k_got, pseudo))
    grads = call(merge_kernel, place, [k_near, k_got, v_near, v_got], [((rows, 2 * HEAD), bf16)] * GROUPS)
    grads_in = back(grads)
    pseudo = after(grads[0], pseudo)
    theta_far = lax.ppermute(pseudo, "island", [(i, i ^ 1) for i in range(islands)])
    d_queries, = unpack(place, after(grads[0], d_queries), 1)
    theta_new, momentum_new = call(
        theta_update_kernel, place, [pseudo, after(d_queries, theta_far), theta_global, momentum],
        [((frag_rows, frag_width), f32)] * 2)
    d_keys, d_values = unpack(place, after(theta_new, grads_in), 2)
    return (context[None], d_queries[None], d_keys[None], d_values[None], theta_new, momentum_new)


def solution(mesh):
    seq = P("island", "fsdp", None)
    return jax.shard_map(
        body,
        mesh=mesh,
        in_specs=(seq, seq, seq, seq, P("island"), P("island"), P("fsdp", None), seq, P("fsdp", None)),
        out_specs=(seq, seq, seq, seq, P("fsdp", None), P("fsdp", None)),
        check_vma=False,
    )
```

```python
import math
import jax
import jax.numpy as jnp
from jax import lax
from jax.experimental import pallas as pl
from jax.experimental.pallas import tpu as pltpu
from jax.sharding import PartitionSpec as P

HEAD = 128
GROUPS = 4
WIDE = 4
COLS = WIDE * HEAD
TILE = 512
NOTE = 16
neg_large = -1e30
score_scale = HEAD ** (-0.5)
exp2_scale = score_scale / math.log(2.0)
outer_momentum = 0.9
outer_rate = 0.7
f32 = jnp.float32
bf16 = jnp.bfloat16


def call(kernel, place, ins, outs, scratch=(), flops=0, exps=0, vmem=63):
    def whole(a):
        zeros = (0,) * len(a.shape)
        return pl.BlockSpec(a.shape, lambda: zeros)

    outs = [jax.ShapeDtypeStruct(s, t) for s, t in outs]
    size = sum(math.prod(a.shape) * a.dtype.itemsize for a in [*ins, *outs])
    return pl.pallas_call(
        kernel,
        in_specs=[pl.BlockSpec(memory_space=pltpu.SMEM)] + [whole(a) for a in ins],
        out_specs=[whole(a) for a in outs],
        out_shape=outs,
        scratch_shapes=[pltpu.VMEM(s, t) for s, t in scratch],
        compiler_params=pltpu.CompilerParams(vmem_limit_bytes=vmem * 2**20),
        cost_estimate=pl.CostEstimate(flops=flops, bytes_accessed=size if flops else 0, transcendentals=exps),
    )(place, *ins)


def after(earlier, later):
    return lax.optimization_barrier((earlier, later))[1]


def at(j):
    return pl.ds(pl.multiple_of(j * TILE, TILE), TILE)


def turn(x):
    return x.astype(f32).T.astype(bf16)


def source(place_ref, r):
    return (place_ref[0] + GROUPS - r) % GROUPS


def key_rows(place_ref, r, other):
    side = place_ref[1]
    block = 2 * source(place_ref, r) + ((1 - side) if other else side)
    return pl.ds(pl.multiple_of(block * (TILE // 2), TILE // 2), TILE // 2)


def lanes(index, width):
    return pl.ds(pl.multiple_of(index * width, width), width)


def extent(place_ref, r, rows):
    side, length = place_ref[1], place_ref[2]
    base = (2 * source(place_ref, r) + side) * rows
    live = (jnp.minimum(base + rows, length) + (TILE - 1)) // TILE
    return base, length, live


def keep_mask(j, base, length, rows):
    key_pos = j * TILE + lax.broadcasted_iota(jnp.int32, (TILE, rows), 0)
    query_pos = base + lax.broadcasted_iota(jnp.int32, (TILE, rows), 1)
    keep = (key_pos <= query_pos) & (key_pos < length)
    return jnp.concatenate([keep] * WIDE, axis=1)


def forward_kernel(place_ref, *refs):
    qg_refs, (near_ref, far_ref), refs = refs[:GROUPS], refs[GROUPS:GROUPS + 2], refs[GROUPS + 2:]
    ctx_refs, (near_out, far_out, stat_ref), refs = refs[:GROUPS], refs[GROUPS:GROUPS + 3], refs[GROUPS + 3:]
    soft, q_cols, g_cols, g_rows, v_cols, kv_ref, dv_ref, acc = refs
    rows = qg_refs[0].shape[0]
    window = kv_ref.shape[0]
    wide = WIDE * rows
    dv_ref[...] = jnp.zeros_like(dv_ref)
    for r in range(GROUPS):
        kv_ref[key_rows(place_ref, r, False), :] = near_ref[r]
        kv_ref[key_rows(place_ref, r, True), :] = far_ref[r]
    for j in range(window // rows):
        span = slice(j * rows, (j + 1) * rows)
        v_cols[:, span] = turn(kv_ref[span, HEAD:])
    for r in range(GROUPS):
        base, length, live = extent(place_ref, r, rows)
        qg_ref = qg_refs[r]
        row_id = base + lax.broadcasted_iota(jnp.int32, (rows, HEAD), 0)
        for h in range(WIDE):
            span = slice(h * rows, (h + 1) * rows)
            g_h = qg_ref[:, COLS + h * HEAD:COLS + (h + 1) * HEAD]
            g_h = jnp.where(row_id < length, g_h.astype(f32), 0.0)
            g_rows[span, :] = g_h.astype(bf16)
            q_cols[:, span] = turn(qg_ref[:, h * HEAD:(h + 1) * HEAD])
            g_cols[:, span] = g_h.T.astype(bf16)

        def score(j):
            return exp2_scale * jnp.dot(kv_ref[at(j), :HEAD], q_cols[...], preferred_element_type=f32)

        def score_full(j, top):
            s = score(j)
            soft[at(j), :] = s
            return jnp.maximum(top, jnp.max(s, axis=0, keepdims=True))

        top = lax.fori_loop(0, live - 1, score_full, jnp.full((1, wide), neg_large, f32))
        s = jnp.where(keep_mask(live - 1, base, length, rows), score(live - 1), neg_large)
        soft[at(live - 1), :] = s
        top = jnp.maximum(top, jnp.max(s, axis=0, keepdims=True))

        def weigh(j, total):
            e = jnp.exp2(soft[at(j), :] - top)
            soft[at(j), :] = e
            return total + jnp.sum(e, axis=0, keepdims=True)

        total = lax.fori_loop(0, live, weigh, jnp.zeros((1, wide), f32))
        inverse = 1.0 / total

        def forward(j, context):
            p = (soft[at(j), :] * inverse).astype(bf16)
            dv_ref[at(j), :] += jnp.dot(p, g_rows[...], preferred_element_type=f32)
            acc[...] += jnp.dot(v_cols[:, at(j)], p, preferred_element_type=f32)
            return context

        acc[...] = jnp.zeros_like(acc)
        lax.fori_loop(0, live, forward, 0)
        context = acc[...]
        stat_ref[r, 0:1, :] = top
        stat_ref[r, 1:2, :] = inverse
        stat_ref[r, 2:3, :] = jnp.sum(g_cols[...].astype(f32) * context, axis=0, keepdims=True)
        for h in range(WIDE):
            ctx_refs[r][:, h * HEAD:(h + 1) * HEAD] = context[:, h * rows:(h + 1) * rows].T.astype(bf16)
    for r in range(GROUPS):
        near_out[r] = dv_ref[key_rows(place_ref, r, False), :]
        far_out[r] = dv_ref[key_rows(place_ref, r, True), :].astype(bf16)


def backward_kernel(place_ref, *refs):
    qg_refs, (near_ref, far_ref, stat_ref), refs = refs[:GROUPS], refs[GROUPS:GROUPS + 3], refs[GROUPS + 3:]
    dq_refs, (near_out, far_out), refs = refs[:GROUPS], refs[GROUPS:GROUPS + 2], refs[GROUPS + 2:]
    q_cols, g_cols, q_rows, k_cols, dq_cols, kv_ref, dk_ref = refs
    rows = qg_refs[0].shape[0]
    window = kv_ref.shape[0]
    dk_ref[...] = jnp.zeros_like(dk_ref)
    for r in range(GROUPS):
        kv_ref[key_rows(place_ref, r, False), :] = near_ref[r]
        kv_ref[key_rows(place_ref, r, True), :] = far_ref[r]
    for j in range(window // rows):
        span = slice(j * rows, (j + 1) * rows)
        k_cols[:, span] = turn(kv_ref[span, :HEAD])
    for r in range(GROUPS):
        base, length, live = extent(place_ref, r, rows)
        qg_ref = qg_refs[r]
        row_id = base + lax.broadcasted_iota(jnp.int32, (rows, HEAD), 0)
        for h in range(WIDE):
            span = slice(h * rows, (h + 1) * rows)
            q_h = qg_ref[:, h * HEAD:(h + 1) * HEAD]
            g_h = qg_ref[:, COLS + h * HEAD:COLS + (h + 1) * HEAD]
            g_h = jnp.where(row_id < length, g_h.astype(f32), 0.0)
            q_rows[span, :] = q_h
            q_cols[:, span] = turn(q_h)
            g_cols[:, span] = g_h.T.astype(bf16)

        def backward(j, edge):
            s = exp2_scale * jnp.dot(kv_ref[at(j), :HEAD], q_cols[...], preferred_element_type=f32)
            if edge:
                s = jnp.where(keep_mask(j, base, length, rows), s, neg_large)
            p = jnp.exp2(s - stat_ref[r, 0:1, :]) * stat_ref[r, 1:2, :]
            d = jnp.dot(kv_ref[at(j), HEAD:], g_cols[...], preferred_element_type=f32)
            d = (p * (d - stat_ref[r, 2:3, :])).astype(bf16)
            dk_ref[at(j), :] += score_scale * jnp.dot(d, q_rows[...], preferred_element_type=f32)
            return jnp.dot(k_cols[:, at(j)], d, preferred_element_type=f32)

        dq_cols[...] = backward(live - 1, True)

        def step(j, carry):
            dq_cols[...] += backward(j, False)
            return carry

        lax.fori_loop(0, live - 1, step, 0)
        for h in range(WIDE):
            dq_refs[r][:, h * HEAD:(h + 1) * HEAD] = (score_scale * dq_cols[:, h * rows:(h + 1) * rows].T).astype(bf16)
    for r in range(GROUPS):
        near_out[r] = dk_ref[key_rows(place_ref, r, False), :]
        far_out[r] = dk_ref[key_rows(place_ref, r, True), :].astype(bf16)


def forward_call(place, blocks, near, far):
    groups, rows, _ = near.shape
    window, wide = 2 * groups * rows, WIDE * rows
    near_part, far_part = ((groups, rows, HEAD), f32), ((groups, rows, HEAD), bf16)
    return call(
        forward_kernel, place, [*blocks, near, far],
        [((rows, COLS), bf16)] * groups + [near_part, far_part, ((groups, 8, wide), f32)],
        [((window, wide), f32), ((HEAD, wide), bf16), ((HEAD, wide), bf16), ((wide, HEAD), bf16), ((HEAD, window), bf16),
         ((window, 2 * HEAD), bf16), ((window, HEAD), f32), ((HEAD, wide), f32)],
        flops=12 * 10**9, exps=10**7, vmem=63)


def backward_call(place, blocks, near, far, stat):
    groups, rows, _ = near.shape
    window, wide = 2 * groups * rows, WIDE * rows
    near_part, far_part = ((groups, rows, HEAD), f32), ((groups, rows, HEAD), bf16)
    return call(
        backward_kernel, place, [*blocks, near, far, stat],
        [((rows, COLS), bf16)] * groups + [near_part, far_part],
        [((HEAD, wide), bf16), ((HEAD, wide), bf16), ((wide, HEAD), bf16), ((HEAD, window), bf16), ((HEAD, wide), f32),
         ((window, 2 * HEAD), bf16), ((window, HEAD), f32)],
        flops=12 * 10**9, exps=10**7, vmem=63)


def pack_pairs_kernel(place_ref, a_ref, b_ref, *out_refs):
    width = a_ref.shape[1] // GROUPS
    for r in range(GROUPS):
        span = lanes((place_ref[0] + r) % GROUPS, width)
        out_refs[r][:, :width] = a_ref[:, span]
        out_refs[r][:, width:] = b_ref[:, span]


def pack_kernel(place_ref, q_ref, g_ref, local_ref, *refs):
    out_refs, sent_ref = refs[:GROUPS], refs[GROUPS]
    pack_pairs_kernel(place_ref, q_ref, g_ref, *out_refs)
    width = sent_ref.shape[2]
    row = lax.broadcasted_iota(jnp.int32, (NOTE, width), 0)
    length, steps = place_ref[2], place_ref[5]
    note = jnp.where(row == 0, steps, jnp.where(row == 1, length // 16, length % 16)).astype(f32).astype(bf16)
    for i in range(sent_ref.shape[0]):
        sent_ref[i, :-NOTE, :] = local_ref[:, i * width:(i + 1) * width]
        sent_ref[i, -NOTE:, :] = note


def pack_pairs(place, k, v):
    rows, width = k.shape
    return call(pack_pairs_kernel, place, [k, v], [((rows, 2 * width // GROUPS), bf16)] * GROUPS)


def pack(place, q, g, local):
    rows, (frag_rows, frag_width) = q.shape[0], local.shape
    return call(
        pack_kernel, place, [q, g, local],
        [((rows, 2 * COLS), bf16)] * GROUPS + [((8, frag_rows + NOTE, frag_width // 8), bf16)])


def unpack_kernel(place_ref, *refs):
    ins, outs = refs[:GROUPS], refs[GROUPS:]
    width = outs[0].shape[1] // GROUPS
    for r in range(GROUPS):
        for i, out in enumerate(outs):
            out[:, lanes((place_ref[0] + r) % GROUPS, width)] = ins[r][:, i * width:(i + 1) * width]


def unpack(place, blocks, count):
    rows, width = blocks[0].shape
    return call(unpack_kernel, place, blocks, [((rows, GROUPS * width // count), bf16)] * count)


def merge_kernel(place_ref, dk_near, dk_far, dv_near, dv_far, *out_refs):
    for r in range(GROUPS):
        out_refs[r][:, :HEAD] = (dk_near[r] + dk_far[r].astype(f32)).astype(bf16)
        out_refs[r][:, HEAD:] = (dv_near[r] + dv_far[r].astype(f32)).astype(bf16)


def theta_sum_kernel(place_ref, g_ref, in_ref, out_ref):
    frag_rows, (count, _, width) = g_ref.shape[0], out_ref.shape
    for part in range(count):
        span = slice(part * width, (part + 1) * width)
        g = g_ref[:, lanes(place_ref[3] * count + part, width)]
        total, drift = 0.0, 0.0
        for i in range(in_ref.shape[0]):
            note = in_ref[i, frag_rows:, span].astype(f32)
            weight = note[0:1, :] * (16.0 * note[1:2, :] + note[2:3, :])
            total = total + weight
            drift = drift + weight * (g - in_ref[i, :frag_rows, span].astype(f32))
        out_ref[part, :frag_rows, :] = drift
        out_ref[part, frag_rows:, :] = jnp.broadcast_to(total, (8, width))


def theta_mean_kernel(place_ref, in_ref, out_ref):
    total = (in_ref[0] + in_ref[1]) + (in_ref[2] + in_ref[3])
    mean = total[:-8] / total[-8:-7]
    for part in range(out_ref.shape[0]):
        out_ref[part] = mean


def theta_update_kernel(place_ref, near_ref, far_ref, g_ref, m_ref, theta_ref, moment_ref):
    count, _, width = near_ref.shape
    for c, ref in ((place_ref[4], near_ref), (1 - place_ref[4], far_ref)):
        for k in range(count):
            y, z = divmod(k, 4)
            span = lanes((2 * y + c) * 4 + z, width)
            pseudo = ref[k]
            moment = outer_momentum * m_ref[:, span] + pseudo
            moment_ref[:, span] = moment
            theta_ref[:, span] = g_ref[:, span] - outer_rate * (pseudo + outer_momentum * moment)


def body(queries, keys, values, d_out, lengths, steps, theta_global, theta_local, momentum):
    rows = queries.shape[1]
    ranks, islands = lax.axis_size("fsdp"), lax.axis_size("island")
    rank = lax.axis_index("fsdp").astype(jnp.int32)
    me = lax.axis_index("island").astype(jnp.int32)
    place = jnp.stack([rank // 2, rank % 2, lengths[0], me % 8, me % 2, steps[0]])

    def along(x, r):
        return x if r == 0 else lax.ppermute(x, "fsdp", [(i, (i + 2 * r) % ranks) for i in range(ranks)])

    def back(blocks):
        return [along(x, -r) for r, x in enumerate(blocks)]

    def across(x):
        return lax.ppermute(x, "fsdp", [(i, i ^ 1) for i in range(ranks)])

    over_y_core = [[8 * z + i for i in range(8)] for z in range(4)]
    over_z = [[8 * z + i for z in range(4)] for i in range(8)]
    over_y = [[8 * z + 2 * y + c for y in range(4)] for z in range(4) for c in range(2)]

    def spread(x, groups):
        return lax.all_to_all(x, "island", 0, 0, axis_index_groups=groups, tiled=True)

    frag_rows, frag_width = theta_global.shape
    line, piece = frag_width // 8, frag_width // 32
    near = [along(x, r) for r, x in enumerate(pack_pairs(place, keys[0], values[0]))]
    near, queries, d_out, theta_local = lax.optimization_barrier((near, queries, d_out, theta_local))
    near = jnp.stack(near)
    far = across(near)
    *blocks, sent = pack(place, queries[0], d_out[0], theta_local[0])
    blocks = [along(x, r) for r, x in enumerate(blocks)]
    drift = spread(sent, over_y_core)
    drift, = call(theta_sum_kernel, place, [theta_global, drift], [((4, frag_rows + 8, piece), f32)])
    blocks, near, far = after(drift, (blocks, near, far))
    drift = spread(drift, over_z)

    *context, v_near, v_far, stat = forward_call(place, blocks, near, far)
    v_far, drift, context, stat = lax.optimization_barrier((v_far, drift, context, stat))
    v_got = across(v_far)
    context = back(context)
    pseudo, = call(theta_mean_kernel, place, [drift], [((4, frag_rows, piece), f32)])
    stat = after(pseudo, stat)
    pseudo = spread(pseudo, over_z)
    *d_queries, k_near, k_far = backward_call(place, blocks, near, far, stat)
    k_far, v_got, context, pseudo = lax.optimization_barrier((k_far, v_got, context, pseudo))
    pseudo = jnp.broadcast_to(pseudo, (4, 4, frag_rows, piece)).reshape(16, frag_rows, piece)
    pseudo = spread(pseudo, over_y)
    k_got = across(k_far)
    d_queries = back(d_queries)
    context = after(d_queries, context)
    context, = unpack(place, context, 1)
    k_got, pseudo = after(context, (k_got, pseudo))
    grads = call(merge_kernel, place, [k_near, k_got, v_near, v_got], [((rows, 2 * HEAD), bf16)] * GROUPS)
    grads_in = back(grads)
    pseudo = after(grads[0], pseudo)
    theta_far = lax.ppermute(pseudo, "island", [(i, i ^ 1) for i in range(islands)])
    d_queries, = unpack(place, after(grads[0], d_queries), 1)
    theta_new, momentum_new = call(
        theta_update_kernel, place, [pseudo, after(d_queries, theta_far), theta_global, momentum],
        [((frag_rows, frag_width), f32)] * 2)
    d_keys, d_values = unpack(place, after(theta_new, grads_in), 2)
    return (context[None], d_queries[None], d_keys[None], d_values[None], theta_new, momentum_new)


def solution(mesh):
    seq = P("island", "fsdp", None)
    return jax.shard_map(
        body,
        mesh=mesh,
        in_specs=(seq, seq, seq, seq, P("island"), P("island"), P("fsdp", None), seq, P("fsdp", None)),
        out_specs=(seq, seq, seq, seq, P("fsdp", None), P("fsdp", None)),
        check_vma=False,
    )
```
